32 devices in a mesh: groups: 2 (over x), brick: 8 (over z, y), chan: 2 (over core).
Axes of the slice: x: 2, y: 2, z: 4, core: 2. Of those that a mesh axis runs over, the one named last changes fastest.
Arguments:
- features: bfloat16 [32, 32768], P('chan', ('groups', 'brick')), parts along dimension 1, may hold values from -6 to 6
- pair_counts: int32 [16, 8], P(('groups', 'brick')), parts along dimension 0, may hold values from 1 to 2048, as said below
- pair_points: int32 [16, 8, 2048], P(('groups', 'brick')), parts along dimension 0, may hold values from 0 to 2047
- pair_cells: int32 [16, 8, 2048], P(('groups', 'brick')), parts along dimension 0, may hold values from 0 to 262143
- enc_weight: float32 [16, 8, 2048], P(('groups', 'brick')), parts along dimension 0, may hold values from 0.2 to 1
- dec_weight: float32 [16, 8, 2048], P(('groups', 'brick')), parts along dimension 0, may hold values from 0.1 to 1
- skip_weight: float32 [32, 32], P('chan'), may hold values from -1 to 1
- spectral_weight: float32 [2, 32, 32, 32, 1024], P(None, 'brick', None, None, 'chan'), may hold values from -2 to 2
- bias: float32 [32], P('chan'), may hold values from -3 to 3
Outputs:
- decoded: float32 [32, 32768], P('chan', ('groups', 'brick')), parts along dimension 1
The draws below stay inside these ranges and needn't reach their ends.
There are 2 independent parts, one for each index of `groups`. The reference program is written for one: setup_inputs(seed, part) draws one part's arguments, and reference() takes and returns one part's arrays. A program takes and returns all parts, laid end to end along the dimension named above; an argument that names none is the same for every part. Nothing has to cross between parts.
Inputs may be any that keep to these rules, and one draw needn't show every extreme that they name: The first pair_counts[s, d] slots of brick s toward slab d hold pairs, the rest are padding. Every brick sends 1 or more pairs to every slab. In every draw one slab receives 2048 pairs from every brick.
All inputs are finite; a program needn't handle non-finite values.
Results may differ from the reference program's by a relative error of at most 0.0015.
Values may be sent and summed in bfloat16 or wider, within the bound.
A program may use at most 448 MiB of HBM per device.

```python
import math
import jax
import jax.numpy as jnp
from jax import lax

C = 32
G = 128
M = 32
PTS_DEV = 2048
CAP = 2048
SLAB = 262144
POINTS = 16384
N_BRICK = 8


def draw_pair_counts(key, part):
    key = jax.random.fold_in(key, 11)
    key_level, key_full, key_minus = jax.random.split(key, 3)
    columns = jnp.arange(N_BRICK, dtype=jnp.int32)[None, :]
    level = jax.random.randint(key_level, (N_BRICK, N_BRICK), 1, 5)
    minus = jax.random.randint(key_minus, (N_BRICK, N_BRICK), 0, CAP // 4)
    counts = CAP * level // 4 - minus
    fullest = jax.random.randint(key_full, (), 0, N_BRICK)
    counts = jnp.where(columns == fullest, CAP, counts)
    return counts.astype(jnp.int32)


def plant(entries, key, smallest, largest):
    longest = entries.shape.index(max(entries.shape))
    spots = []
    for shift in (0, 1):
        where = [jax.random.randint(jax.random.fold_in(key, axis), (), 0, length) for axis, length in enumerate(entries.shape)]
        where[longest] = (where[longest] + shift) % entries.shape[longest]
        spots.append(tuple(where))
    return entries.at[spots[0]].set(smallest).at[spots[1]].set(largest)


def level_of(rng, dims, cuts, low, top_value):
    def one(axis_at, shards_of):
        draws = jax.random.uniform(jax.random.fold_in(jax.random.fold_in(rng, 6), axis_at), (shards_of,), jnp.float32, low / len(cuts), top_value / len(cuts))
        return jnp.repeat(jnp.exp(draws), dims[axis_at] // shards_of).reshape((-1,) + (1,) * (len(dims) - axis_at - 1))

    loudness = one(*cuts[0])
    for cut in cuts[1:]:
        loudness = loudness * one(*cut)
    return loudness


def normal_values(stream_key, dims, spread, limit, cuts=(), kind=jnp.bfloat16):
    loudness = level_of(stream_key, dims, cuts, -0.22, 0.18) if cuts else 1.0
    array = jax.random.normal(stream_key, dims, jnp.float32) * spread * loudness
    return jnp.minimum(jnp.maximum(array, -limit), limit).astype(kind)


def setup_inputs(seed: int = 0, part: int = 0) -> dict:
    key_list = jax.random.split(jax.random.key(seed), 10)
    own_keys = jax.random.split(jax.random.fold_in(key_list[9], part), 10)
    features = normal_values(own_keys[0], (C, POINTS), 1.0, 6.0, ((0, 2), (1, 8)))
    pair_counts = draw_pair_counts(jax.random.fold_in(jax.random.fold_in(key_list[9], part), 71), part)
    pair_points = plant(jax.random.randint(own_keys[2], (N_BRICK, N_BRICK, CAP), 0, PTS_DEV), jax.random.fold_in(own_keys[2], 1), 0, PTS_DEV - 1).astype(jnp.int32)
    pair_cells = plant(jax.random.randint(own_keys[3], (N_BRICK, N_BRICK, CAP), 0, SLAB), jax.random.fold_in(own_keys[3], 1), 0, SLAB - 1).astype(jnp.int32)
    enc_weight = jnp.clip(0.2 + 0.8 * jax.random.uniform(own_keys[4], (N_BRICK, N_BRICK, CAP), jnp.float32) ** level_of(own_keys[4], (N_BRICK, N_BRICK, CAP), ((0, 8),), -0.2, 0.2), 0.2, 1.0)
    dec_weight = jnp.clip(jnp.exp(math.log(1.0) - 2.3025851 * jax.random.uniform(own_keys[5], (N_BRICK, N_BRICK, CAP), jnp.float32) ** level_of(own_keys[5], (N_BRICK, N_BRICK, CAP), ((0, 8),), -0.2, 0.2)), 0.1, 1.0)
    skip_weight = normal_values(key_list[6], (C, C), C ** -0.5, 1.0, ((0, 2),), jnp.float32)
    spectral_weight = normal_values(key_list[7], (2, M, C, C, M * M), (C // 4) ** -0.5, 2.0, ((1, 8), (4, 2)), jnp.float32)
    bias = normal_values(key_list[8], (C,), 0.5, 3.0, ((0, 2),), jnp.float32)
    return {"features": features, "pair_counts": pair_counts, "pair_points": pair_points, "pair_cells": pair_cells, "enc_weight": enc_weight, "dec_weight": dec_weight, "skip_weight": skip_weight, "spectral_weight": spectral_weight, "bias": bias}


def reference(features, pair_counts, pair_points, pair_cells, enc_weight, dec_weight, skip_weight, spectral_weight, bias):
    slots = jnp.arange(CAP, dtype=jnp.int32)
    valid = (slots[None, None, :] < pair_counts[:, :, None]).astype(jnp.float32)
    sources = jnp.arange(N_BRICK, dtype=jnp.int32)
    point_index = (sources[:, None, None] * PTS_DEV + pair_points).astype(jnp.int32).reshape(-1)
    cell_index = (sources[None, :, None] * SLAB + pair_cells).astype(jnp.int32).reshape(-1)
    enc_coef = (valid * enc_weight).reshape(-1)
    dec_coef = (valid * dec_weight).reshape(-1)
    feats = features.astype(jnp.float32)
    contrib = feats[:, point_index] * enc_coef[None, :]
    latent = jnp.zeros((C, G * G * G), jnp.float32).at[:, cell_index].add(contrib)
    skip = jnp.dot(skip_weight, latent, precision=lax.Precision.HIGHEST, preferred_element_type=jnp.float32)
    select = jnp.concatenate([jnp.arange(M // 2), jnp.arange(G - M // 2, G)]).astype(jnp.int32)
    zmodes = jnp.arange(M, dtype=jnp.int32)
    scale = 1.0 / (G * math.sqrt(G))

    def forward(channel):
        spectrum = jnp.fft.fftn(channel.reshape(G, G, G))
        return spectrum[select][:, select][:, :, :M]
    coeff = lax.map(forward, latent) * scale
    coeff_re = jnp.real(coeff)
    coeff_im = jnp.imag(coeff)
    weights = spectral_weight.reshape(2, M, C, C, M, M)
    factor = jnp.where(zmodes == 0, 1.0, 2.0)

    def one_output(out_chan):
        w_re = weights[0][:, :, out_chan]
        w_im = weights[1][:, :, out_chan]
        hi = lax.Precision.HIGHEST
        mixed_re = jnp.einsum('bika,iabk->abk', w_re, coeff_re, precision=hi) - jnp.einsum('bika,iabk->abk', w_im, coeff_im, precision=hi)
        mixed_im = jnp.einsum('bika,iabk->abk', w_re, coeff_im, precision=hi) + jnp.einsum('bika,iabk->abk', w_im, coeff_re, precision=hi)
        placed = (mixed_re + 1j * mixed_im) * factor[None, None, :]
        full = jnp.zeros((G, G, G), dtype=placed.dtype)
        full = full.at[select[:, None, None], select[None, :, None], zmodes[None, None, :]].set(placed)
        field = jnp.real(jnp.fft.ifftn(full)) * (G * G * G) * scale
        return field.reshape(-1)
    spectral = lax.map(one_output, jnp.arange(C, dtype=jnp.int32))
    hidden = jax.nn.gelu(spectral + skip + bias[:, None], approximate=True).astype(jnp.bfloat16)
    rows = hidden[:, cell_index].astype(jnp.float32) * dec_coef[None, :]
    decoded = jnp.zeros((C, N_BRICK * PTS_DEV), jnp.float32).at[:, point_index].add(rows)
    return decoded
```

```python
import math

import jax
import jax.numpy as jnp
import numpy as np
from jax import lax
from jax.experimental import pallas as pl
from jax.experimental.pallas import tpu as pltpu
from jax.sharding import PartitionSpec as P

C = 32
G = 128
M = 32
F32 = jnp.float32
BF16 = jnp.bfloat16
NT = (((1,), (1,)), ((), ()))


def angles(freqs, signed):
    places = np.arange(G)
    modes = np.arange(freqs)
    if signed:
        modes = np.where(modes < freqs // 2, modes, modes - freqs + G)
    angle = (modes[:, None] * places[None, :] % G) * (2.0 * math.pi / G)
    return np.cos(angle), np.sin(angle)


def params(mib=48):
    return pltpu.CompilerParams(
        dimension_semantics=("arbitrary",), vmem_limit_bytes=mib * 1024 * 1024
    )


def mm(a, b):
    return jnp.dot(a, b, preferred_element_type=F32)


def hot(index, rows):
    places = lax.broadcasted_iota(jnp.int32, (rows, index.shape[1]), 0)
    return jnp.where(places == index, 1.0, 0.0).astype(BF16)


def pick_kernel(chans, high, table_ref, points_ref, out_ref):
    points = points_ref[...]
    rows = mm(table_ref[...], hot(points & 127, 128)).reshape(chans, high, points.shape[1])
    keep = lax.broadcasted_iota(jnp.int32, (1, high, points.shape[1]), 1) == (points >> 7)[None]
    out_ref[...] = jnp.sum(jnp.where(keep, rows, 0.0), axis=1).astype(BF16)


def pick(features, points, step=1024):
    chans, count = features.shape
    high = count // 128
    total = points.shape[1]
    return pl.pallas_call(
        lambda *r: pick_kernel(chans, high, *r),
        grid=(total // step,),
        in_specs=[
            pl.BlockSpec((chans * high, 128), lambda i: (0, 0)),
            pl.BlockSpec((1, step), lambda i: (0, i)),
        ],
        out_specs=pl.BlockSpec((chans, step), lambda i: (0, i)),
        out_shape=jax.ShapeDtypeStruct((chans, total), BF16),
        compiler_params=params(),
    )(features.reshape(chans * high, 128), points)


def y_phases(tab_ref, y):
    both = mm(tab_ref[...], hot(y, G))
    return both[: 2 * M] + both[2 * M :]


def forward_kernel(chans, width, wins, span_ref, feat_ref, coef_ref, cell_ref, ytab_ref, ztab_ref, out_ref, acc_ref):
    step = pl.program_id(0)

    @pl.when(step == 0)
    def _():
        acc_ref[...] = jnp.zeros_like(acc_ref)

    first, last = span_ref[0, step], span_ref[1, step]
    planes = width * wins

    @pl.when(first < planes)
    def _():
        cells = cell_ref[...]
        x = cells >> 14
        count = cells.shape[1]
        ys = y_phases(ytab_ref, (cells >> 7) & 127)
        zs = mm(ztab_ref[...], hot(cells & 127, G))
        feats = feat_ref[...].astype(F32) * coef_ref[...]
        left = (feats[:, None, :] * ys[None]).astype(BF16).reshape(chans * 2 * M, count)
        for win in range(wins):
            @pl.when((first < (win + 1) * width) & (last >= win * width))
            def _():
                pieces = []
                for part in range(4):
                    piece = zs[part * 16 : part * 16 + 16]
                    for off in range(width):
                        pieces.append(jnp.where(x == win * width + off, piece, 0.0))
                right = jnp.concatenate(pieces, axis=0).astype(BF16)
                acc_ref[win] += lax.dot_general(left, right, NT, preferred_element_type=F32)

    @pl.when(step == pl.num_programs(0) - 1)
    def _():
        half = 2 * width * 16
        for win in range(wins):
            full = acc_ref[win].reshape(chans, 2 * M, 2 * half)
            out_ref[0, win] = (full[:, :M, :half] - full[:, M:, half:]).astype(BF16)
            out_ref[1, win] = (-full[:, :M, half:] - full[:, M:, :half]).astype(BF16)


def forward(feats, coef, cells, span, planes, step):
    chans, total = feats.shape
    width = min(8, planes)
    wins = planes // width
    y_cos, y_sin = angles(M, True)
    z_cos, z_sin = angles(M, False)
    ytab = np.concatenate([y_cos, y_sin]).astype(np.float32)
    yhi = ytab.astype(BF16)
    ylo = (ytab - yhi.astype(np.float32)).astype(BF16)
    ytab = jnp.asarray(np.concatenate([yhi, ylo]))
    ztab = jnp.asarray(np.concatenate([z_cos, z_sin]).astype(BF16))
    lanes = 2 * width * 16
    return pl.pallas_call(
        lambda *r: forward_kernel(chans, width, wins, *r),
        grid_spec=pltpu.PrefetchScalarGridSpec(
            num_scalar_prefetch=1,
            grid=(total // step,),
            in_specs=[
                pl.BlockSpec((chans, step), lambda i, s: (0, i)),
                pl.BlockSpec((1, step), lambda i, s: (0, i)),
                pl.BlockSpec((1, step), lambda i, s: (0, i)),
                pl.BlockSpec((4 * M, G), lambda i, s: (0, 0)),
                pl.BlockSpec((2 * M, G), lambda i, s: (0, 0)),
            ],
            out_specs=pl.BlockSpec((2, wins, chans, M, lanes), lambda i, s: (0, 0, 0, 0, 0)),
            scratch_shapes=[pltpu.VMEM((wins, chans * 2 * M, 2 * lanes), F32)],
        ),
        out_shape=jax.ShapeDtypeStruct((2, wins, chans, M, lanes), BF16),
        compiler_params=params(),
    )(span, feats, coef, cells, ytab, ztab)


def skip_kernel(lists, per, wide, bounds_ref, rounds_ref, mine_ref, cells_ref, vals_ref, w_ref, out_ref):
    step = pl.program_id(0)
    mine = mine_ref[...]
    lanes = 128

    def one(turn, acc):
        hits = []
        vals = []
        for src in range(lists):
            for off in range(wide):
                at = bounds_ref[step, 2 * src] + turn * wide + off
                live = at < bounds_ref[step, 2 * src + 1]
                row = src * per + jnp.where(live, at, 0)
                other = jnp.where(live, cells_ref[pl.ds(row, 1), :], -1)
                hits.append(jnp.where(mine == other, 1.0, 0.0).astype(BF16))
                vals.append(vals_ref[row])
        hit = jnp.concatenate(hits, axis=1)
        val = jnp.concatenate(vals, axis=1)
        return acc + lax.dot_general(val, hit, NT, preferred_element_type=F32)

    acc = lax.fori_loop(0, rounds_ref[step], one, jnp.zeros((2 * C, lanes), F32))
    latent = acc[:C] + acc[C:]
    out_ref[...] = jnp.dot(
        w_ref[...], latent, precision=lax.Precision.HIGHEST, preferred_element_type=F32
    )


def skip_at(feats, coef, cells, weight, lists, slots, slab_cells, wide=2):
    total = cells.shape[1]
    per = slots // 128
    chunks = total // 128
    vals = feats.astype(F32) * coef
    hi = lax.reduce_precision(vals, 8, 7)
    lo = (vals - hi).astype(BF16)
    both = jnp.concatenate([hi.astype(BF16), lo], axis=0)
    both = both.reshape(2 * C, chunks, 128).transpose(1, 0, 2)
    rows = cells.reshape(chunks, 128)
    low = rows[:, 0]
    high = jnp.minimum(rows[:, 127], slab_cells - 1)
    q_low = low.reshape(1, lists, per)
    q_high = rows[:, 127].reshape(1, lists, per)
    start = jnp.sum((q_high < low[:, None, None]).astype(jnp.int32), axis=2)
    end = jnp.sum((q_low <= high[:, None, None]).astype(jnp.int32), axis=2)
    end = jnp.where(low[:, None] >= slab_cells, start, jnp.maximum(end, start))
    rounds = jnp.max((end - start + wide - 1) // wide, axis=1)
    bounds = jnp.stack([start, end], axis=2).reshape(chunks, 2 * lists)
    return pl.pallas_call(
        lambda *r: skip_kernel(lists, per, wide, *r),
        grid_spec=pltpu.PrefetchScalarGridSpec(
            num_scalar_prefetch=2,
            grid=(chunks,),
            in_specs=[
                pl.BlockSpec((128, 1), lambda i, a, b: (i, 0)),
                pl.BlockSpec((chunks, 128), lambda i, a, b: (0, 0)),
                pl.BlockSpec((chunks, 2 * C, 128), lambda i, a, b: (0, 0, 0)),
                pl.BlockSpec(weight.shape, lambda i, a, b: (0, 0)),
            ],
            out_specs=pl.BlockSpec((weight.shape[0], 128), lambda i, a, b: (0, i)),
        ),
        out_shape=jax.ShapeDtypeStruct((weight.shape[0], total), F32),
        compiler_params=params(),
    )(bounds, rounds, cells.reshape(total, 1), rows, both, weight)


def inverse_kernel(chans, width, wins, span_ref, cell_ref, skip_ref, bias_ref, r_ref, ytab_ref, ztab_ref, out_ref, acc_ref):
    step = pl.program_id(0)
    first, last = span_ref[0, step], span_ref[1, step]
    planes = width * wins

    @pl.when(first >= planes)
    def _():
        out_ref[...] = jnp.zeros_like(out_ref)

    @pl.when(first < planes)
    def _():
        cells = cell_ref[...]
        count = cells.shape[1]
        x = cells >> 14
        acc_ref[...] = jnp.zeros_like(acc_ref)
        zs = mm(ztab_ref[...], hot(cells & 127, G))
        for win in range(wins):
            @pl.when((first < (win + 1) * width) & (last >= win * width))
            def _():
                pieces = [jnp.where(x == win * width + off, zs, 0.0) for off in range(width)]
                right = jnp.concatenate(pieces, axis=0).astype(BF16)
                acc_ref[...] += mm(r_ref[win], right)
        ys = y_phases(ytab_ref, (cells >> 7) & 127)
        field = jnp.sum(acc_ref[...].reshape(chans, 2 * M, count) * ys[None], axis=1)
        v = field * (1.0 / (G * math.sqrt(G))) + skip_ref[...] + bias_ref[...]
        out_ref[...] = jax.nn.gelu(v, approximate=True).astype(BF16)


def inverse(cells, skip, bias, mat, span, planes, step):
    chans, total = skip.shape
    width = min(4, planes)
    wins = planes // width
    y_cos, y_sin = angles(M, True)
    z_cos, z_sin = angles(M, False)
    ytab = np.concatenate([y_cos, y_sin]).astype(np.float32)
    yhi = ytab.astype(BF16)
    ylo = (ytab - yhi.astype(np.float32)).astype(BF16)
    ytab = jnp.asarray(np.concatenate([yhi, ylo]))
    factor = np.where(np.arange(M) == 0, 1.0, 2.0)[:, None]
    ztab = jnp.asarray(np.concatenate([z_cos * factor, z_sin * factor]).astype(BF16))
    return pl.pallas_call(
        lambda *r: inverse_kernel(chans, width, wins, *r),
        grid_spec=pltpu.PrefetchScalarGridSpec(
            num_scalar_prefetch=1,
            grid=(total // step,),
            in_specs=[
                pl.BlockSpec((1, step), lambda i, s: (0, i)),
                pl.BlockSpec((chans, step), lambda i, s: (0, i)),
                pl.BlockSpec((chans, 1), lambda i, s: (0, 0)),
                pl.BlockSpec(mat.shape, lambda i, s: (0, 0, 0)),
                pl.BlockSpec((4 * M, G), lambda i, s: (0, 0)),
                pl.BlockSpec((2 * M, G), lambda i, s: (0, 0)),
            ],
            out_specs=pl.BlockSpec((chans, step), lambda i, s: (0, i)),
            scratch_shapes=[pltpu.VMEM((chans * 2 * M, step), F32)],
        ),
        out_shape=jax.ShapeDtypeStruct((chans, total), BF16),
        compiler_params=params(),
    )(span, cells, skip, bias[:, None], mat, ytab, ztab)


def decode_kernel(chans, high, hid_ref, coef_ref, points_ref, out_ref):
    @pl.when(pl.program_id(0) == 0)
    def _():
        out_ref[...] = jnp.zeros_like(out_ref)

    points = points_ref[...]
    count = points.shape[1]
    vals = hid_ref[...].astype(F32) * coef_ref[...]
    hi = vals.astype(BF16).astype(F32)
    lo = vals - hi
    keep = lax.broadcasted_iota(jnp.int32, (1, high, count), 1) == (points >> 7)[None]
    low_hot = hot(points & 127, 128)
    total = jnp.zeros((chans * high, 128), F32)
    for part in (hi, lo):
        spread = jnp.where(keep, part[:, None, :], 0.0).astype(BF16).reshape(chans * high, count)
        total += lax.dot_general(spread, low_hot, NT, preferred_element_type=F32)
    out_ref[...] += total


def decode(hidden, coef, points, count, step=1024):
    chans, total = hidden.shape
    high = count // 128
    out = pl.pallas_call(
        lambda *r: decode_kernel(chans, high, *r),
        grid=(total // step,),
        in_specs=[
            pl.BlockSpec((chans, step), lambda i: (0, i)),
            pl.BlockSpec((1, step), lambda i: (0, i)),
            pl.BlockSpec((1, step), lambda i: (0, i)),
        ],
        out_specs=pl.BlockSpec((chans * high, 128), lambda i: (0, 0)),
        out_shape=jax.ShapeDtypeStruct((chans * high, 128), F32),
        compiler_params=params(),
    )(hidden, coef, points)
    return out.reshape(chans, count)


def shards(
    features,
    pair_counts,
    pair_points,
    pair_cells,
    enc_weight,
    dec_weight,
    skip_weight,
    spectral_weight,
    bias,
):
    bricks = lax.axis_size("brick")
    pair = lax.axis_size("chan")
    chans, point_count = features.shape
    slots = pair_points.shape[-1]
    planes = G // bricks
    slab_cells = planes * G * G
    step = 256
    both = ("brick", "chan")

    valid = jnp.arange(slots, dtype=jnp.int32)[None, :] < pair_counts[0][:, None]
    key = jnp.where(valid, pair_cells[0], slab_cells)
    enc = jnp.where(valid, enc_weight[0], 0.0)
    dec = jnp.where(valid, dec_weight[0], 0.0)
    key, points, enc, dec = lax.sort(
        (key, pair_points[0], enc, dec), dimension=1, num_keys=1, is_stable=False
    )
    points = points.reshape(1, -1)
    picked = pick(features, points)

    meta = jnp.stack([key.astype(F32), enc], axis=1)
    meta = lax.all_to_all(meta, "brick", split_axis=0, concat_axis=0, tiled=True)
    cells = meta[:, 0].astype(jnp.int32).reshape(1, -1)
    coef = meta[:, 1].reshape(1, -1)
    got = lax.all_to_all(
        picked.reshape(chans, bricks, slots), "brick", split_axis=1, concat_axis=1, tiled=True
    ).reshape(chans, -1)
    every = lax.all_gather(got, "chan", axis=0, tiled=True)

    by_step = cells.reshape(-1, step) >> 14
    span = jnp.stack([by_step[:, 0], by_step[:, -1]])
    spec = forward(got, coef, cells, span, planes, step)

    wins = spec.shape[1]
    width = planes // wins
    modes = M // bricks
    kz = M // pair
    sent = spec.reshape(2, wins, chans, bricks, modes, pair, width * kz)
    sent = sent.transpose(3, 5, 0, 1, 4, 2, 6).reshape(bricks * pair, 2, wins, modes, chans, width * kz)
    pencil = lax.all_to_all(sent, both, split_axis=0, concat_axis=0, tiled=True)
    pencil = pencil.reshape(bricks, pair, 2, wins, modes, chans, width, kz)
    pencil = pencil.transpose(4, 1, 5, 7, 2, 0, 3, 6).reshape(modes, C, kz, 2 * G)

    scale = 1.0 / (G * math.sqrt(G))
    x_cos, x_sin = angles(M, True)
    x_cos, x_sin = x_cos.T, x_sin.T
    ahead = np.stack([np.concatenate([x_cos, x_sin]), np.concatenate([-x_sin, x_cos])])
    ahead = jnp.asarray(ahead.astype(BF16))
    coeff = jnp.einsum("bikx,rxa->rbika", pencil, ahead, preferred_element_type=F32) * scale
    coeff = coeff.reshape(2, modes, C, kz * M)
    c_real, c_imag = coeff[0], coeff[1]
    w_real, w_imag = spectral_weight[0], spectral_weight[1]
    m_real = jnp.sum(w_real * c_real[:, :, None] - w_imag * c_imag[:, :, None], axis=1)
    m_imag = jnp.sum(w_real * c_imag[:, :, None] + w_imag * c_real[:, :, None], axis=1)
    mixed = jnp.stack([m_real, m_imag]).astype(BF16).reshape(2, modes, C, kz, M)
    back = np.stack([np.stack([x_cos, -x_sin]), np.stack([x_sin, x_cos])])
    back = jnp.asarray(back.astype(BF16))
    lines = jnp.einsum("sboka,rsxa->rbokx", mixed, back, preferred_element_type=F32).astype(BF16)
    lines = lines.reshape(2, modes, pair, chans, kz, bricks, planes)
    lines = lines.transpose(5, 2, 0, 1, 3, 4, 6).reshape(bricks * pair, 2, modes, chans, kz * planes)
    lines = lax.all_to_all(lines, both, split_axis=0, concat_axis=0, tiled=True)
    lines = lines.reshape(bricks, pair, 2, modes, chans, kz, planes)
    wide = min(4, planes)
    lines = lines.reshape(bricks, pair, 2, modes, chans, kz, planes // wide, wide)
    lines = lines.transpose(2, 6, 4, 0, 3, 7, 1, 5).reshape(2, planes // wide, chans, M, wide, M)
    r_real, r_imag = lines[0], lines[1]
    top = jnp.stack([r_real, -r_imag], axis=4)
    low = jnp.stack([-r_imag, -r_real], axis=4)
    mat = jnp.stack([top, low], axis=2).reshape(planes // wide, chans * 2 * M, wide * 2 * M)

    skip = skip_at(every, coef, cells, skip_weight, bricks, slots, slab_cells)
    hidden = inverse(cells, skip, bias, mat, span, planes, step)
    answered = lax.all_to_all(
        hidden.reshape(chans, bricks, slots), "brick", split_axis=1, concat_axis=1, tiled=True
    )
    return decode(answered.reshape(chans, -1), dec.reshape(1, -1), points, point_count)


def solution(mesh):
    return jax.shard_map(
        shards,
        mesh=mesh,
        in_specs=(
            P("chan", ("groups", "brick")),
            P(("groups", "brick"), None),
            P(("groups", "brick"), None, None),
            P(("groups", "brick"), None, None),
            P(("groups", "brick"), None, None),
            P(("groups", "brick"), None, None),
            P("chan", None),
            P(None, "brick", None, None, "chan"),
            P("chan"),
        ),
        out_specs=P("chan", ("groups", "brick")),
        check_vma=False,
    )
```

```python
import math

import jax
import jax.numpy as jnp
import numpy as np
from jax import lax
from jax.experimental import pallas as pl
from jax.experimental.pallas import tpu as pltpu
from jax.sharding import PartitionSpec as P

C = 32
G = 128
M = 32
F32 = jnp.float32
BF16 = jnp.bfloat16
NT = (((1,), (1,)), ((), ()))


def angles(freqs, signed):
    places = np.arange(G)
    modes = np.arange(freqs)
    if signed:
        modes = np.where(modes < freqs // 2, modes, modes - freqs + G)
    angle = (modes[:, None] * places[None, :] % G) * (2.0 * math.pi / G)
    return np.cos(angle), np.sin(angle)


def params(mib=48):
    return pltpu.CompilerParams(
        dimension_semantics=("arbitrary",), vmem_limit_bytes=mib * 1024 * 1024
    )


def mm(a, b):
    return jnp.dot(a, b, preferred_element_type=F32)


def hot(index, rows):
    places = lax.broadcasted_iota(jnp.int32, (rows, index.shape[1]), 0)
    return jnp.where(places == index, 1.0, 0.0).astype(BF16)


def pick_kernel(chans, high, table_ref, points_ref, out_ref):
    points = points_ref[...]
    rows = mm(table_ref[...], hot(points & 127, 128)).reshape(chans, high, points.shape[1])
    keep = lax.broadcasted_iota(jnp.int32, (1, high, points.shape[1]), 1) == (points >> 7)[None]
    out_ref[...] = jnp.sum(jnp.where(keep, rows, 0.0), axis=1).astype(BF16)


def pick(features, points, step=1024):
    chans, count = features.shape
    high = count // 128
    total = points.shape[1]
    return pl.pallas_call(
        lambda *r: pick_kernel(chans, high, *r),
        grid=(total // step,),
        in_specs=[
            pl.BlockSpec((chans * high, 128), lambda i: (0, 0)),
            pl.BlockSpec((1, step), lambda i: (0, i)),
        ],
        out_specs=pl.BlockSpec((chans, step), lambda i: (0, i)),
        out_shape=jax.ShapeDtypeStruct((chans, total), BF16),
        compiler_params=params(),
    )(features.reshape(chans * high, 128), points)


def y_phases(tab_ref, y):
    both = mm(tab_ref[...], hot(y, G))
    return both[: 2 * M] + both[2 * M :]


def forward_kernel(chans, width, wins, span_ref, feat_ref, coef_ref, cell_ref, ytab_ref, ztab_ref, out_ref, acc_ref):
    step = pl.program_id(0)

    @pl.when(step == 0)
    def _():
        acc_ref[...] = jnp.zeros_like(acc_ref)

    first, last = span_ref[0, step], span_ref[1, step]
    planes = width * wins

    @pl.when(first < planes)
    def _():
        cells = cell_ref[...]
        x = cells >> 14
        count = cells.shape[1]
        ys = y_phases(ytab_ref, (cells >> 7) & 127)
        zs = mm(ztab_ref[...], hot(cells & 127, G))
        feats = feat_ref[...].astype(F32) * coef_ref[...]
        left = (feats[:, None, :] * ys[None]).astype(BF16).reshape(chans * 2 * M, count)
        for win in range(wins):
            @pl.when((first < (win + 1) * width) & (last >= win * width))
            def _():
                pieces = []
                for part in range(4):
                    piece = zs[part * 16 : part * 16 + 16]
                    for off in range(width):
                        pieces.append(jnp.where(x == win * width + off, piece, 0.0))
                right = jnp.concatenate(pieces, axis=0).astype(BF16)
                acc_ref[win] += lax.dot_general(left, right, NT, preferred_element_type=F32)

    @pl.when(step == pl.num_programs(0) - 1)
    def _():
        half = 2 * width * 16
        for win in range(wins):
            full = acc_ref[win].reshape(chans, 2 * M, 2 * half)
            out_ref[0, win] = (full[:, :M, :half] - full[:, M:, half:]).astype(BF16)
            out_ref[1, win] = (-full[:, :M, half:] - full[:, M:, :half]).astype(BF16)


def forward(feats, coef, cells, span, planes, step):
    chans, total = feats.shape
    width = min(8, planes)
    wins = planes // width
    y_cos, y_sin = angles(M, True)
    z_cos, z_sin = angles(M, False)
    ytab = np.concatenate([y_cos, y_sin]).astype(np.float32)
    yhi = ytab.astype(BF16)
    ylo = (ytab - yhi.astype(np.float32)).astype(BF16)
    ytab = jnp.asarray(np.concatenate([yhi, ylo]))
    ztab = jnp.asarray(np.concatenate([z_cos, z_sin]).astype(BF16))
    lanes = 2 * width * 16
    return pl.pallas_call(
        lambda *r: forward_kernel(chans, width, wins, *r),
        grid_spec=pltpu.PrefetchScalarGridSpec(
            num_scalar_prefetch=1,
            grid=(total // step,),
            in_specs=[
                pl.BlockSpec((chans, step), lambda i, s: (0, i)),
                pl.BlockSpec((1, step), lambda i, s: (0, i)),
                pl.BlockSpec((1, step), lambda i, s: (0, i)),
                pl.BlockSpec((4 * M, G), lambda i, s: (0, 0)),
                pl.BlockSpec((2 * M, G), lambda i, s: (0, 0)),
            ],
            out_specs=pl.BlockSpec((2, wins, chans, M, lanes), lambda i, s: (0, 0, 0, 0, 0)),
            scratch_shapes=[pltpu.VMEM((wins, chans * 2 * M, 2 * lanes), F32)],
        ),
        out_shape=jax.ShapeDtypeStruct((2, wins, chans, M, lanes), BF16),
        compiler_params=params(),
    )(span, feats, coef, cells, ytab, ztab)


def skip_kernel(chans, group, count_ref, work_ref, mine_ref, cells_ref, vals_ref, out_ref):
    live = count_ref[pl.program_id(0)]
    mine = mine_ref[...]

    def one(turn, acc):
        hits = []
        vals = []
        for off in range(group):
            at = turn * group + off
            row = work_ref[0, 0, at]
            other = jnp.where(at < live, cells_ref[pl.ds(row, 1), :], -1)
            hits.append(jnp.where(mine == other, 1.0, 0.0).astype(BF16))
            vals.append(vals_ref[row])
        hit = jnp.concatenate(hits, axis=1)
        val = jnp.concatenate(vals, axis=0)
        return acc + mm(hit, val)

    rounds = (live + group - 1) // group
    acc = lax.fori_loop(0, rounds, one, jnp.zeros((128, 2 * chans), F32))
    rows = lax.broadcasted_iota(jnp.int32, (chans, 2 * chans), 0)
    cols = lax.broadcasted_iota(jnp.int32, (chans, 2 * chans), 1)
    fold = jnp.where((cols == rows) | (cols == rows + chans), 1.0, 0.0)
    out_ref[...] = lax.dot_general(
        fold, acc, NT, precision=lax.Precision.HIGHEST, preferred_element_type=F32
    )


def skip_at(feats, coef, cells, weight, slab_cells, group=8):
    chans = weight.shape[0]
    total = cells.shape[1]
    chunks = total // 128
    vals = jnp.einsum(
        "in,oi->no",
        feats.astype(F32) * coef,
        weight,
        precision=lax.Precision.HIGHEST,
        preferred_element_type=F32,
    )
    hi = lax.reduce_precision(vals, 8, 7)
    both = jnp.concatenate([hi, vals - hi], axis=1).astype(BF16).reshape(chunks, 128, 2 * chans)
    rows = cells.reshape(chunks, 128)
    low = rows[:, 0]
    top = rows[:, 127]
    high = jnp.minimum(top, slab_cells - 1)
    meets = (top[None] >= low[:, None]) & (low[None] <= high[:, None])
    meets &= low[:, None] < slab_cells
    places = jnp.arange(chunks, dtype=jnp.int32)
    work = lax.sort(jnp.where(meets, places[None], chunks - 1), dimension=1)
    count = jnp.sum(meets.astype(jnp.int32), axis=1)
    return pl.pallas_call(
        lambda *r: skip_kernel(chans, group, *r),
        grid_spec=pltpu.PrefetchScalarGridSpec(
            num_scalar_prefetch=1,
            grid=(chunks,),
            in_specs=[
                pl.BlockSpec((1, 1, chunks), lambda i, a: (i, 0, 0), memory_space=pltpu.SMEM),
                pl.BlockSpec((128, 1), lambda i, a: (i, 0)),
                pl.BlockSpec((chunks, 128), lambda i, a: (0, 0)),
                pl.BlockSpec((chunks, 128, 2 * chans), lambda i, a: (0, 0, 0)),
            ],
            out_specs=pl.BlockSpec((chans, 128), lambda i, a: (0, i)),
        ),
        out_shape=jax.ShapeDtypeStruct((chans, total), F32),
        compiler_params=params(),
    )(count, work.reshape(chunks, 1, chunks), cells.reshape(total, 1), rows, both)


def ahead_kernel(pair, wins, in_ref, mat_ref, out_ref, acc_ref):
    step = pl.program_id(0)
    _, _, _, _, modes, chans, lanes = in_ref.shape
    rows = []
    for src in range(pair):
        parts = [
            in_ref[0, src, s, win].reshape(modes * chans, lanes) for s in range(2) for win in range(wins)
        ]
        rows.append(jnp.concatenate(parts, axis=1))
    part = mm(jnp.concatenate(rows, axis=0), mat_ref[0])

    @pl.when(step == 0)
    def _():
        acc_ref[...] = part

    @pl.when(step > 0)
    def _():
        acc_ref[...] += part

    @pl.when(step == pl.num_programs(0) - 1)
    def _():
        half = acc_ref.shape[1] // 2
        full = acc_ref[...] * (1.0 / (G * math.sqrt(G)))
        full = full.reshape(pair, modes, chans, 2 * half)
        for src in range(pair):
            for s in range(2):
                out_ref[s, :, src * chans : (src + 1) * chans, :] = full[
                    src, :, :, s * half : (s + 1) * half
                ]


def x_matrices(bricks, kz):
    planes = G // bricks
    x_cos, x_sin = angles(M, True)
    x_cos = x_cos.reshape(M, bricks, planes)
    x_sin = x_sin.reshape(M, bricks, planes)
    eye = np.eye(kz)
    ahead = np.zeros((bricks, 2, planes, kz, 2, kz, M), np.float32)
    back = np.zeros((bricks, 2, kz, M, 2, planes, kz), np.float32)
    for s, r, table in ((0, 0, x_cos), (1, 0, x_sin), (0, 1, -x_sin), (1, 1, x_cos)):
        ahead[:, s, :, :, r] = np.einsum("aBx,kq->Bxkqa", table, eye)
        back[:, r, :, :, s] = np.einsum("aBx,kq->Bkaxq", table, eye)
    side = 2 * planes * kz
    return (
        jnp.asarray(ahead.reshape(bricks, side, 2 * kz * M).astype(BF16)),
        jnp.asarray(back.reshape(bricks, 2 * kz * M, side).astype(BF16)),
    )


def ahead_x(pencil, mat):
    bricks, pair, _, wins, modes, chans, lanes = pencil.shape
    side, cols = mat.shape[1:]
    return pl.pallas_call(
        lambda *r: ahead_kernel(pair, wins, *r),
        grid=(bricks,),
        in_specs=[
            pl.BlockSpec((1,) + pencil.shape[1:], lambda i: (i, 0, 0, 0, 0, 0, 0)),
            pl.BlockSpec((1, side, cols), lambda i: (i, 0, 0)),
        ],
        out_specs=pl.BlockSpec((2, modes, pair * chans, cols // 2), lambda i: (0, 0, 0, 0)),
        out_shape=jax.ShapeDtypeStruct((2, modes, pair * chans, cols // 2), F32),
        scratch_shapes=[pltpu.VMEM((pair * modes * chans, cols), F32)],
        compiler_params=params(),
    )(pencil, mat)


def back_kernel(pair, real_ref, imag_ref, mat_ref, out_ref):
    modes, outs, lanes = real_ref.shape
    chans = outs // pair
    left = jnp.concatenate(
        [real_ref[...].reshape(modes * outs, lanes), imag_ref[...].reshape(modes * outs, lanes)], axis=1
    ).astype(BF16)
    res = mm(left, mat_ref[0])
    half = res.shape[1] // 2
    res = res.reshape(modes, pair, chans, 2 * half)
    for dest in range(pair):
        for s in range(2):
            piece = res[:, dest, :, s * half : (s + 1) * half]
            out_ref[0, dest, s] = piece.reshape(modes * chans, half).astype(BF16)


def back_x(real, imag, mat, pair):
    bricks, rows, side = mat.shape
    modes, outs, lanes = real.shape
    shape = (bricks, pair, 2, modes * outs // pair, side // 2)
    return pl.pallas_call(
        lambda *r: back_kernel(pair, *r),
        grid=(bricks,),
        in_specs=[
            pl.BlockSpec(real.shape, lambda i: (0, 0, 0)),
            pl.BlockSpec(real.shape, lambda i: (0, 0, 0)),
            pl.BlockSpec((1, rows, side), lambda i: (i, 0, 0)),
        ],
        out_specs=pl.BlockSpec((1,) + shape[1:], lambda i: (i, 0, 0, 0, 0)),
        out_shape=jax.ShapeDtypeStruct(shape, BF16),
        compiler_params=params(),
    )(real, imag, mat)


def inverse_kernel(pair, width, wins, span_ref, cell_ref, skip_ref, bias_ref, r_ref, ytab_ref, ztab_ref, out_ref, mat_ref, acc_ref):
    step = pl.program_id(0)
    first, last = span_ref[0, step], span_ref[1, step]
    planes = width * wins
    kz = M // pair
    rows = r_ref.shape[2]
    lanes = width * kz
    chans = out_ref.shape[0]

    @pl.when(step == 0)
    def _():
        for win in range(wins):
            for src in range(r_ref.shape[0] // pair):
                parts = [
                    r_ref[src * pair + half, s, :, win * lanes : (win + 1) * lanes]
                    for s in range(2)
                    for half in range(pair)
                ]
                mat_ref[win, src * rows : (src + 1) * rows, :] = jnp.concatenate(parts, axis=1)

    @pl.when(first >= planes)
    def _():
        out_ref[...] = jnp.zeros_like(out_ref)

    @pl.when(first < planes)
    def _():
        cells = cell_ref[...]
        count = cells.shape[1]
        x = cells >> 14
        acc_ref[...] = jnp.zeros_like(acc_ref)
        zs = -mm(ztab_ref[...], hot(cells & 127, G))
        for win in range(wins):
            @pl.when((first < (win + 1) * width) & (last >= win * width))
            def _():
                masks = [x == win * width + off for off in range(width)]
                sides = []
                for s in range(2):
                    pieces = []
                    for half in range(pair):
                        at = s * M + half * kz
                        pieces += [jnp.where(mask, zs[at : at + kz], 0.0) for mask in masks]
                    sides.append(jnp.concatenate(pieces, axis=0).astype(BF16))
                mat = mat_ref[win]
                acc_ref[0] += mm(mat, jnp.concatenate([-sides[0], sides[1]], axis=0))
                acc_ref[1] += mm(mat, jnp.concatenate([sides[1], sides[0]], axis=0))
        ys = y_phases(ytab_ref, (cells >> 7) & 127)
        field = jnp.zeros((chans, count), F32)
        for s in range(2):
            for b in range(M):
                at = s * M + b
                field += acc_ref[s, b * chans : (b + 1) * chans, :] * ys[at : at + 1]
        v = field * (1.0 / (G * math.sqrt(G))) + skip_ref[...] + bias_ref[...]
        out_ref[...] = jax.nn.gelu(v, approximate=True).astype(BF16)


def inverse(cells, skip, bias, lines, span, planes, pair, step):
    chans, total = skip.shape
    width = min(8, planes)
    wins = planes // width
    y_cos, y_sin = angles(M, True)
    z_cos, z_sin = angles(M, False)
    ytab = np.concatenate([y_cos, y_sin]).astype(np.float32)
    yhi = ytab.astype(BF16)
    ylo = (ytab - yhi.astype(np.float32)).astype(BF16)
    ytab = jnp.asarray(np.concatenate([yhi, ylo]))
    factor = np.where(np.arange(M) == 0, 1.0, 2.0)[:, None]
    ztab = jnp.asarray(np.concatenate([z_cos * factor, z_sin * factor]).astype(BF16))
    return pl.pallas_call(
        lambda *r: inverse_kernel(pair, width, wins, *r),
        grid_spec=pltpu.PrefetchScalarGridSpec(
            num_scalar_prefetch=1,
            grid=(total // step,),
            in_specs=[
                pl.BlockSpec((1, step), lambda i, s: (0, i)),
                pl.BlockSpec((chans, step), lambda i, s: (0, i)),
                pl.BlockSpec((chans, 1), lambda i, s: (0, 0)),
                pl.BlockSpec(lines.shape, lambda i, s: (0, 0, 0, 0)),
                pl.BlockSpec((4 * M, G), lambda i, s: (0, 0)),
                pl.BlockSpec((2 * M, G), lambda i, s: (0, 0)),
            ],
            out_specs=pl.BlockSpec((chans, step), lambda i, s: (0, i)),
            scratch_shapes=[
                pltpu.VMEM((wins, M * chans, 2 * width * M), BF16),
                pltpu.VMEM((2, M * chans, step), F32),
            ],
        ),
        out_shape=jax.ShapeDtypeStruct((chans, total), BF16),
        compiler_params=params(),
    )(span, cells, skip, bias[:, None], lines, ytab, ztab)


def decode_kernel(chans, high, hid_ref, coef_ref, points_ref, out_ref):
    @pl.when(pl.program_id(0) == 0)
    def _():
        out_ref[...] = jnp.zeros_like(out_ref)

    points = points_ref[...]
    count = points.shape[1]
    vals = hid_ref[...].astype(F32) * coef_ref[...]
    hi = vals.astype(BF16).astype(F32)
    lo = vals - hi
    keep = lax.broadcasted_iota(jnp.int32, (1, high, count), 1) == (points >> 7)[None]
    low_hot = hot(points & 127, 128)
    total = jnp.zeros((chans * high, 128), F32)
    for part in (hi, lo):
        spread = jnp.where(keep, part[:, None, :], 0.0).astype(BF16).reshape(chans * high, count)
        total += lax.dot_general(spread, low_hot, NT, preferred_element_type=F32)
    out_ref[...] += total


def decode(hidden, coef, points, count, step=1024):
    chans, total = hidden.shape
    high = count // 128
    out = pl.pallas_call(
        lambda *r: decode_kernel(chans, high, *r),
        grid=(total // step,),
        in_specs=[
            pl.BlockSpec((chans, step), lambda i: (0, i)),
            pl.BlockSpec((1, step), lambda i: (0, i)),
            pl.BlockSpec((1, step), lambda i: (0, i)),
        ],
        out_specs=pl.BlockSpec((chans * high, 128), lambda i: (0, 0)),
        out_shape=jax.ShapeDtypeStruct((chans * high, 128), F32),
        compiler_params=params(),
    )(hidden, coef, points)
    return out.reshape(chans, count)


def shards(
    features,
    pair_counts,
    pair_points,
    pair_cells,
    enc_weight,
    dec_weight,
    skip_weight,
    spectral_weight,
    bias,
):
    bricks = lax.axis_size("brick")
    pair = lax.axis_size("chan")
    chans, point_count = features.shape
    slots = pair_points.shape[-1]
    planes = G // bricks
    slab_cells = planes * G * G
    step = 256
    both = ("brick", "chan")

    valid = jnp.arange(slots, dtype=jnp.int32)[None, :] < pair_counts[0][:, None]
    key = jnp.where(valid, pair_cells[0], slab_cells)
    enc = jnp.where(valid, enc_weight[0], 0.0)
    dec = jnp.where(valid, dec_weight[0], 0.0)
    key, points, enc, dec = lax.sort(
        (key, pair_points[0], enc, dec), dimension=1, num_keys=1, is_stable=False
    )
    points = points.reshape(1, -1)
    picked = pick(features, points)

    meta = jnp.stack([key.astype(F32), enc], axis=1)
    meta = lax.all_to_all(meta, "brick", split_axis=0, concat_axis=0, tiled=True)
    cells = meta[:, 0].astype(jnp.int32).reshape(1, -1)
    coef = meta[:, 1].reshape(1, -1)
    got = lax.all_to_all(
        picked.reshape(chans, bricks, slots), "brick", split_axis=1, concat_axis=1, tiled=True
    ).reshape(chans, -1)
    every = lax.all_gather(got, "chan", axis=0, tiled=True)

    by_step = cells.reshape(-1, step) >> 14
    span = jnp.stack([by_step[:, 0], by_step[:, -1]])
    spec = forward(got, coef, cells, span, planes, step)

    wins = spec.shape[1]
    width = planes // wins
    modes = M // bricks
    kz = M // pair
    sent = spec.reshape(2, wins, chans, bricks, modes, pair, width * kz)
    sent = sent.transpose(3, 5, 0, 1, 4, 2, 6).reshape(bricks * pair, 2, wins, modes, chans, width * kz)
    pencil = lax.all_to_all(sent, both, split_axis=0, concat_axis=0, tiled=True)
    pencil = pencil.reshape(bricks, pair, 2, wins, modes, chans, width * kz)
    ahead, back = x_matrices(bricks, kz)
    coeff = ahead_x(pencil, ahead)
    c_real, c_imag = coeff[0], coeff[1]
    w_real, w_imag = spectral_weight[0], spectral_weight[1]
    m_real = jnp.sum(w_real * c_real[:, :, None] - w_imag * c_imag[:, :, None], axis=1)
    m_imag = jnp.sum(w_real * c_imag[:, :, None] + w_imag * c_real[:, :, None], axis=1)
    lines = back_x(m_real, m_imag, back, pair)
    lines = lines.reshape((bricks * pair,) + lines.shape[2:])
    lines = lax.all_to_all(lines, both, split_axis=0, concat_axis=0, tiled=True)

    skip = skip_at(every, coef, cells, skip_weight, slab_cells)
    hidden = inverse(cells, skip, bias, lines, span, planes, pair, step)
    answered = lax.all_to_all(
        hidden.reshape(chans, bricks, slots), "brick", split_axis=1, concat_axis=1, tiled=True
    )
    return decode(answered.reshape(chans, -1), dec.reshape(1, -1), points, point_count)


def solution(mesh):
    return jax.shard_map(
        shards,
        mesh=mesh,
        in_specs=(
            P("chan", ("groups", "brick")),
            P(("groups", "brick"), None),
            P(("groups", "brick"), None, None),
            P(("groups", "brick"), None, None),
            P(("groups", "brick"), None, None),
            P(("groups", "brick"), None, None),
            P("chan", None),
            P(None, "brick", None, None, "chan"),
            P("chan"),
        ),
        out_specs=P("chan", ("groups", "brick")),
        check_vma=False,
    )
```

```python
import math

import jax
import jax.numpy as jnp
import numpy as np
from jax import lax
from jax.experimental import pallas as pl
from jax.experimental.pallas import tpu as pltpu
from jax.sharding import PartitionSpec as P

C = 32
G = 128
M = 32
F32 = jnp.float32
BF16 = jnp.bfloat16
NT = (((1,), (1,)), ((), ()))


def angles(freqs, signed):
    places = np.arange(G)
    modes = np.arange(freqs)
    if signed:
        modes = np.where(modes < freqs // 2, modes, modes - freqs + G)
    angle = (modes[:, None] * places[None, :] % G) * (2.0 * math.pi / G)
    return np.cos(angle), np.sin(angle)


def params(mib=48):
    return pltpu.CompilerParams(
        dimension_semantics=("arbitrary",), vmem_limit_bytes=mib * 1024 * 1024
    )


def mm(a, b):
    return jnp.dot(a, b, preferred_element_type=F32)


def hot(index, rows):
    places = lax.broadcasted_iota(jnp.int32, (rows, index.shape[1]), 0)
    return jnp.where(places == index, 1.0, 0.0).astype(BF16)


def pick_kernel(chans, high, table_ref, points_ref, out_ref):
    points = points_ref[...]
    rows = mm(table_ref[...], hot(points & 127, 128)).reshape(chans, high, points.shape[1])
    keep = lax.broadcasted_iota(jnp.int32, (1, high, points.shape[1]), 1) == (points >> 7)[None]
    out_ref[...] = jnp.sum(jnp.where(keep, rows, 0.0), axis=1).astype(BF16)


def pick(features, points, step=1024):
    chans, count = features.shape
    high = count // 128
    total = points.shape[1]
    return pl.pallas_call(
        lambda *r: pick_kernel(chans, high, *r),
        grid=(total // step,),
        in_specs=[
            pl.BlockSpec((chans * high, 128), lambda i: (0, 0)),
            pl.BlockSpec((1, step), lambda i: (0, i)),
        ],
        out_specs=pl.BlockSpec((chans, step), lambda i: (0, i)),
        out_shape=jax.ShapeDtypeStruct((chans, total), BF16),
        compiler_params=params(),
    )(features.reshape(chans * high, 128), points)


def y_phases(tab_ref, y):
    both = mm(tab_ref[...], hot(y, G))
    return both[: 2 * M] + both[2 * M :]


def forward_kernel(chans, width, wins, span_ref, feat_ref, coef_ref, cell_ref, ytab_ref, ztab_ref, out_ref, acc_ref):
    step = pl.program_id(0)

    @pl.when(step == 0)
    def _():
        acc_ref[...] = jnp.zeros_like(acc_ref)

    first, last = span_ref[0, step], span_ref[1, step]
    planes = width * wins

    @pl.when(first < planes)
    def _():
        cells = cell_ref[...]
        x = cells >> 14
        count = cells.shape[1]
        ys = y_phases(ytab_ref, (cells >> 7) & 127)
        zs = mm(ztab_ref[...], hot(cells & 127, G))
        feats = feat_ref[...].astype(F32) * coef_ref[...]
        left = (feats[:, None, :] * ys[None]).astype(BF16).reshape(chans * 2 * M, count)
        for win in range(wins):
            @pl.when((first < (win + 1) * width) & (last >= win * width))
            def _():
                pieces = []
                for part in range(4):
                    piece = zs[part * 16 : part * 16 + 16]
                    for off in range(width):
                        pieces.append(jnp.where(x == win * width + off, piece, 0.0))
                right = jnp.concatenate(pieces, axis=0).astype(BF16)
                acc_ref[win] += lax.dot_general(left, right, NT, preferred_element_type=F32)

    @pl.when(step == pl.num_programs(0) - 1)
    def _():
        half = 2 * width * 16
        for win in range(wins):
            full = acc_ref[win].reshape(chans, 2 * M, 2 * half)
            out_ref[0, win] = (full[:, :M, :half] - full[:, M:, half:]).astype(BF16)
            out_ref[1, win] = (-full[:, :M, half:] - full[:, M:, :half]).astype(BF16)


def forward(feats, coef, cells, span, planes, step):
    chans, total = feats.shape
    width = min(8, planes)
    wins = planes // width
    y_cos, y_sin = angles(M, True)
    z_cos, z_sin = angles(M, False)
    ytab = np.concatenate([y_cos, y_sin]).astype(np.float32)
    yhi = ytab.astype(BF16)
    ylo = (ytab - yhi.astype(np.float32)).astype(BF16)
    ytab = jnp.asarray(np.concatenate([yhi, ylo]))
    ztab = jnp.asarray(np.concatenate([z_cos, z_sin]).astype(BF16))
    lanes = 2 * width * 16
    return pl.pallas_call(
        lambda *r: forward_kernel(chans, width, wins, *r),
        grid_spec=pltpu.PrefetchScalarGridSpec(
            num_scalar_prefetch=1,
            grid=(total // step,),
            in_specs=[
                pl.BlockSpec((chans, step), lambda i, s: (0, i)),
                pl.BlockSpec((1, step), lambda i, s: (0, i)),
                pl.BlockSpec((1, step), lambda i, s: (0, i)),
                pl.BlockSpec((4 * M, G), lambda i, s: (0, 0)),
                pl.BlockSpec((2 * M, G), lambda i, s: (0, 0)),
            ],
            out_specs=pl.BlockSpec((2, wins, chans, M, lanes), lambda i, s: (0, 0, 0, 0, 0)),
            scratch_shapes=[pltpu.VMEM((wins, chans * 2 * M, 2 * lanes), F32)],
        ),
        out_shape=jax.ShapeDtypeStruct((2, wins, chans, M, lanes), BF16),
        compiler_params=params(),
    )(span, feats, coef, cells, ytab, ztab)


def skip_kernel(chans, group, batch, count_ref, work_ref, cells_ref, vals_ref, out_ref):
    rows = lax.broadcasted_iota(jnp.int32, (chans, 2 * chans), 0)
    cols = lax.broadcasted_iota(jnp.int32, (chans, 2 * chans), 1)
    fold = jnp.where((cols == rows) | (cols == rows + chans), 1.0, 0.0)
    for part in range(batch):
        chunk = pl.program_id(0) * batch + part
        live = count_ref[chunk]
        mine = jnp.transpose(jnp.broadcast_to(cells_ref[pl.ds(chunk, 1), :], (128, 128)))

        def one(turn, acc):
            hits = []
            vals = []
            for off in range(group):
                at = turn * group + off
                row = work_ref[part, 0, at]
                other = jnp.where(at < live, cells_ref[pl.ds(row, 1), :], -1)
                hits.append(jnp.where(mine == other, 1.0, 0.0).astype(BF16))
                vals.append(vals_ref[row])
            hit = jnp.concatenate(hits, axis=1)
            val = jnp.concatenate(vals, axis=0)
            return acc + mm(hit, val)

        rounds = (live + group - 1) // group
        acc = lax.fori_loop(0, rounds, one, jnp.zeros((128, 2 * chans), F32))
        out_ref[:, part * 128 : (part + 1) * 128] = lax.dot_general(
            fold, acc, NT, precision=lax.Precision.HIGHEST, preferred_element_type=F32
        )


def skip_at(feats, coef, cells, weight, slab_cells, group=8, batch=8):
    chans = weight.shape[0]
    total = cells.shape[1]
    chunks = total // 128
    vals = jnp.einsum(
        "in,oi->no",
        feats.astype(F32) * coef,
        weight,
        precision=lax.Precision.HIGHEST,
        preferred_element_type=F32,
    )
    hi = lax.reduce_precision(vals, 8, 7)
    both = jnp.concatenate([hi, vals - hi], axis=1).astype(BF16).reshape(chunks, 128, 2 * chans)
    rows = cells.reshape(chunks, 128)
    low = rows[:, 0]
    top = rows[:, 127]
    high = jnp.minimum(top, slab_cells - 1)
    meets = (top[None] >= low[:, None]) & (low[None] <= high[:, None])
    meets &= low[:, None] < slab_cells
    places = jnp.arange(chunks, dtype=jnp.int32)
    work = lax.sort(jnp.where(meets, places[None], chunks - 1), dimension=1)
    count = jnp.sum(meets.astype(jnp.int32), axis=1)
    return pl.pallas_call(
        lambda *r: skip_kernel(chans, group, batch, *r),
        grid_spec=pltpu.PrefetchScalarGridSpec(
            num_scalar_prefetch=1,
            grid=(chunks // batch,),
            in_specs=[
                pl.BlockSpec((batch, 1, chunks), lambda i, a: (i, 0, 0), memory_space=pltpu.SMEM),
                pl.BlockSpec((chunks, 128), lambda i, a: (0, 0)),
                pl.BlockSpec((chunks, 128, 2 * chans), lambda i, a: (0, 0, 0)),
            ],
            out_specs=pl.BlockSpec((chans, batch * 128), lambda i, a: (0, i)),
        ),
        out_shape=jax.ShapeDtypeStruct((chans, total), F32),
        compiler_params=params(),
    )(count, work.reshape(chunks, 1, chunks), rows, both)


def ahead_kernel(pair, wins, in_ref, mat_ref, out_ref, acc_ref):
    step = pl.program_id(0)
    _, _, _, _, modes, chans, lanes = in_ref.shape
    rows = []
    for src in range(pair):
        parts = [
            in_ref[0, src, s, win].reshape(modes * chans, lanes) for s in range(2) for win in range(wins)
        ]
        rows.append(jnp.concatenate(parts, axis=1))
    part = mm(jnp.concatenate(rows, axis=0), mat_ref[0])

    @pl.when(step == 0)
    def _():
        acc_ref[...] = part

    @pl.when(step > 0)
    def _():
        acc_ref[...] += part

    @pl.when(step == pl.num_programs(0) - 1)
    def _():
        half = acc_ref.shape[1] // 2
        full = acc_ref[...] * (1.0 / (G * math.sqrt(G)))
        full = full.reshape(pair, modes, chans, 2 * half)
        for src in range(pair):
            for s in range(2):
                out_ref[s, :, src * chans : (src + 1) * chans, :] = full[
                    src, :, :, s * half : (s + 1) * half
                ]


def x_matrices(bricks, kz):
    planes = G // bricks
    x_cos, x_sin = angles(M, True)
    x_cos = x_cos.reshape(M, bricks, planes)
    x_sin = x_sin.reshape(M, bricks, planes)
    eye = np.eye(kz)
    ahead = np.zeros((bricks, 2, planes, kz, 2, kz, M), np.float32)
    back = np.zeros((bricks, 2, kz, M, 2, planes, kz), np.float32)
    for s, r, table in ((0, 0, x_cos), (1, 0, x_sin), (0, 1, -x_sin), (1, 1, x_cos)):
        ahead[:, s, :, :, r] = np.einsum("aBx,kq->Bxkqa", table, eye)
        back[:, r, :, :, s] = np.einsum("aBx,kq->Bkaxq", table, eye)
    side = 2 * planes * kz
    return (
        jnp.asarray(ahead.reshape(bricks, side, 2 * kz * M).astype(BF16)),
        jnp.asarray(back.reshape(bricks, 2 * kz * M, side).astype(BF16)),
    )


def ahead_x(pencil, mat):
    bricks, pair, _, wins, modes, chans, lanes = pencil.shape
    side, cols = mat.shape[1:]
    return pl.pallas_call(
        lambda *r: ahead_kernel(pair, wins, *r),
        grid=(bricks,),
        in_specs=[
            pl.BlockSpec((1,) + pencil.shape[1:], lambda i: (i, 0, 0, 0, 0, 0, 0)),
            pl.BlockSpec((1, side, cols), lambda i: (i, 0, 0)),
        ],
        out_specs=pl.BlockSpec((2, modes, pair * chans, cols // 2), lambda i: (0, 0, 0, 0)),
        out_shape=jax.ShapeDtypeStruct((2, modes, pair * chans, cols // 2), F32),
        scratch_shapes=[pltpu.VMEM((pair * modes * chans, cols), F32)],
        compiler_params=params(),
    )(pencil, mat)


def back_kernel(pair, real_ref, imag_ref, mat_ref, out_ref):
    modes, outs, lanes = real_ref.shape
    chans = outs // pair
    left = jnp.concatenate(
        [real_ref[...].reshape(modes * outs, lanes), imag_ref[...].reshape(modes * outs, lanes)], axis=1
    ).astype(BF16)
    res = mm(left, mat_ref[0])
    half = res.shape[1] // 2
    res = res.reshape(modes, pair, chans, 2 * half)
    for dest in range(pair):
        for s in range(2):
            piece = res[:, dest, :, s * half : (s + 1) * half]
            out_ref[0, dest, s] = piece.reshape(modes * chans, half).astype(BF16)


def back_x(real, imag, mat, pair):
    bricks, rows, side = mat.shape
    modes, outs, lanes = real.shape
    shape = (bricks, pair, 2, modes * outs // pair, side // 2)
    return pl.pallas_call(
        lambda *r: back_kernel(pair, *r),
        grid=(bricks,),
        in_specs=[
            pl.BlockSpec(real.shape, lambda i: (0, 0, 0)),
            pl.BlockSpec(real.shape, lambda i: (0, 0, 0)),
            pl.BlockSpec((1, rows, side), lambda i: (i, 0, 0)),
        ],
        out_specs=pl.BlockSpec((1,) + shape[1:], lambda i: (i, 0, 0, 0, 0)),
        out_shape=jax.ShapeDtypeStruct(shape, BF16),
        compiler_params=params(),
    )(real, imag, mat)


def inverse_kernel(pair, width, wins, span_ref, cell_ref, skip_ref, bias_ref, r_ref, ytab_ref, ztab_ref, out_ref, mat_ref, acc_ref):
    step = pl.program_id(0)
    first, last = span_ref[0, step], span_ref[1, step]
    planes = width * wins
    kz = M // pair
    rows = r_ref.shape[2]
    lanes = width * kz
    chans = out_ref.shape[0]

    @pl.when(step == 0)
    def _():
        for win in range(wins):
            for src in range(r_ref.shape[0] // pair):
                parts = [
                    r_ref[src * pair + half, s, :, win * lanes : (win + 1) * lanes]
                    for s in range(2)
                    for half in range(pair)
                ]
                mat_ref[win, src * rows : (src + 1) * rows, :] = jnp.concatenate(parts, axis=1)

    @pl.when(first >= planes)
    def _():
        out_ref[...] = jnp.zeros_like(out_ref)

    @pl.when(first < planes)
    def _():
        cells = cell_ref[...]
        count = cells.shape[1]
        x = cells >> 14
        acc_ref[...] = jnp.zeros_like(acc_ref)
        zs = -mm(ztab_ref[...], hot(cells & 127, G))
        for win in range(wins):
            @pl.when((first < (win + 1) * width) & (last >= win * width))
            def _():
                masks = [x == win * width + off for off in range(width)]
                sides = []
                for s in range(2):
                    pieces = []
                    for half in range(pair):
                        at = s * M + half * kz
                        pieces += [jnp.where(mask, zs[at : at + kz], 0.0) for mask in masks]
                    sides.append(jnp.concatenate(pieces, axis=0).astype(BF16))
                mat = mat_ref[win]
                acc_ref[0] += mm(mat, jnp.concatenate([-sides[0], sides[1]], axis=0))
                acc_ref[1] += mm(mat, jnp.concatenate([sides[1], sides[0]], axis=0))
        ys = y_phases(ytab_ref, (cells >> 7) & 127)
        field = jnp.zeros((chans, count), F32)
        for s in range(2):
            for b in range(M):
                at = s * M + b
                field += acc_ref[s, b * chans : (b + 1) * chans, :] * ys[at : at + 1]
        v = field * (1.0 / (G * math.sqrt(G))) + skip_ref[...] + bias_ref[...]
        out_ref[...] = jax.nn.gelu(v, approximate=True).astype(BF16)


def inverse(cells, skip, bias, lines, span, planes, pair, step):
    chans, total = skip.shape
    width = min(8, planes)
    wins = planes // width
    y_cos, y_sin = angles(M, True)
    z_cos, z_sin = angles(M, False)
    ytab = np.concatenate([y_cos, y_sin]).astype(np.float32)
    yhi = ytab.astype(BF16)
    ylo = (ytab - yhi.astype(np.float32)).astype(BF16)
    ytab = jnp.asarray(np.concatenate([yhi, ylo]))
    factor = np.where(np.arange(M) == 0, 1.0, 2.0)[:, None]
    ztab = jnp.asarray(np.concatenate([z_cos * factor, z_sin * factor]).astype(BF16))
    return pl.pallas_call(
        lambda *r: inverse_kernel(pair, width, wins, *r),
        grid_spec=pltpu.PrefetchScalarGridSpec(
            num_scalar_prefetch=1,
            grid=(total // step,),
            in_specs=[
                pl.BlockSpec((1, step), lambda i, s: (0, i)),
                pl.BlockSpec((chans, step), lambda i, s: (0, i)),
                pl.BlockSpec((chans, 1), lambda i, s: (0, 0)),
                pl.BlockSpec(lines.shape, lambda i, s: (0, 0, 0, 0)),
                pl.BlockSpec((4 * M, G), lambda i, s: (0, 0)),
                pl.BlockSpec((2 * M, G), lambda i, s: (0, 0)),
            ],
            out_specs=pl.BlockSpec((chans, step), lambda i, s: (0, i)),
            scratch_shapes=[
                pltpu.VMEM((wins, M * chans, 2 * width * M), BF16),
                pltpu.VMEM((2, M * chans, step), F32),
            ],
        ),
        out_shape=jax.ShapeDtypeStruct((chans, total), BF16),
        compiler_params=params(),
    )(span, cells, skip, bias[:, None], lines, ytab, ztab)


def decode_kernel(chans, high, hid_ref, coef_ref, points_ref, out_ref):
    @pl.when(pl.program_id(0) == 0)
    def _():
        out_ref[...] = jnp.zeros_like(out_ref)

    points = points_ref[...]
    count = points.shape[1]
    vals = hid_ref[...].astype(F32) * coef_ref[...]
    hi = vals.astype(BF16).astype(F32)
    lo = vals - hi
    keep = lax.broadcasted_iota(jnp.int32, (1, high, count), 1) == (points >> 7)[None]
    low_hot = hot(points & 127, 128)
    total = jnp.zeros((chans * high, 128), F32)
    for part in (hi, lo):
        spread = jnp.where(keep, part[:, None, :], 0.0).astype(BF16).reshape(chans * high, count)
        total += lax.dot_general(spread, low_hot, NT, preferred_element_type=F32)
    out_ref[...] += total


def decode(hidden, coef, points, count, step=1024):
    chans, total = hidden.shape
    high = count // 128
    out = pl.pallas_call(
        lambda *r: decode_kernel(chans, high, *r),
        grid=(total // step,),
        in_specs=[
            pl.BlockSpec((chans, step), lambda i: (0, i)),
            pl.BlockSpec((1, step), lambda i: (0, i)),
            pl.BlockSpec((1, step), lambda i: (0, i)),
        ],
        out_specs=pl.BlockSpec((chans * high, 128), lambda i: (0, 0)),
        out_shape=jax.ShapeDtypeStruct((chans * high, 128), F32),
        compiler_params=params(),
    )(hidden, coef, points)
    return out.reshape(chans, count)


def shards(
    features,
    pair_counts,
    pair_points,
    pair_cells,
    enc_weight,
    dec_weight,
    skip_weight,
    spectral_weight,
    bias,
):
    bricks = lax.axis_size("brick")
    pair = lax.axis_size("chan")
    chans, point_count = features.shape
    slots = pair_points.shape[-1]
    planes = G // bricks
    slab_cells = planes * G * G
    step = 256
    both = ("brick", "chan")

    valid = jnp.arange(slots, dtype=jnp.int32)[None, :] < pair_counts[0][:, None]
    key = jnp.where(valid, pair_cells[0], slab_cells)
    enc = jnp.where(valid, enc_weight[0], 0.0)
    dec = jnp.where(valid, dec_weight[0], 0.0)
    key, points, enc, dec = lax.sort(
        (key, pair_points[0], enc, dec), dimension=1, num_keys=1, is_stable=False
    )
    points = points.reshape(1, -1)
    picked = pick(features, points)

    meta = jnp.stack([key.astype(F32), enc], axis=1)
    meta = lax.all_to_all(meta, "brick", split_axis=0, concat_axis=0, tiled=True)
    cells = meta[:, 0].astype(jnp.int32).reshape(1, -1)
    coef = meta[:, 1].reshape(1, -1)
    got = lax.all_to_all(
        picked.reshape(chans, bricks, slots), "brick", split_axis=1, concat_axis=1, tiled=True
    ).reshape(chans, -1)
    every = lax.all_gather(got, "chan", axis=0, tiled=True)

    by_step = cells.reshape(-1, step) >> 14
    span = jnp.stack([by_step[:, 0], by_step[:, -1]])
    spec = forward(got, coef, cells, span, planes, step)

    wins = spec.shape[1]
    width = planes // wins
    modes = M // bricks
    kz = M // pair
    sent = spec.reshape(2, wins, chans, bricks, modes, pair, width * kz)
    sent = sent.transpose(3, 5, 0, 1, 4, 2, 6).reshape(bricks * pair, 2, wins, modes, chans, width * kz)
    pencil = lax.all_to_all(sent, both, split_axis=0, concat_axis=0, tiled=True)
    pencil = pencil.reshape(bricks, pair, 2, wins, modes, chans, width * kz)
    ahead, back = x_matrices(bricks, kz)
    coeff = ahead_x(pencil, ahead)
    c_real, c_imag = coeff[0], coeff[1]
    w_real, w_imag = spectral_weight[0], spectral_weight[1]
    m_real = jnp.sum(w_real * c_real[:, :, None] - w_imag * c_imag[:, :, None], axis=1)
    m_imag = jnp.sum(w_real * c_imag[:, :, None] + w_imag * c_real[:, :, None], axis=1)
    lines = back_x(m_real, m_imag, back, pair)
    lines = lines.reshape((bricks * pair,) + lines.shape[2:])
    lines = lax.all_to_all(lines, both, split_axis=0, concat_axis=0, tiled=True)

    skip = skip_at(every, coef, cells, skip_weight, slab_cells)
    hidden = inverse(cells, skip, bias, lines, span, planes, pair, step)
    answered = lax.all_to_all(
        hidden.reshape(chans, bricks, slots), "brick", split_axis=1, concat_axis=1, tiled=True
    )
    return decode(answered.reshape(chans, -1), dec.reshape(1, -1), points, point_count)


def solution(mesh):
    return jax.shard_map(
        shards,
        mesh=mesh,
        in_specs=(
            P("chan", ("groups", "brick")),
            P(("groups", "brick"), None),
            P(("groups", "brick"), None, None),
            P(("groups", "brick"), None, None),
            P(("groups", "brick"), None, None),
            P(("groups", "brick"), None, None),
            P("chan", None),
            P(None, "brick", None, None, "chan"),
            P("chan"),
        ),
        out_specs=P("chan", ("groups", "brick")),
        check_vma=False,
    )
```
